512 devices in a mesh: dp: 32 (over x_hi, z), test: 16 (over y, x_lo, core).
Axes of the slice: x: 4 (x_hi: 2, x_lo: 2; x = x_hi * 2 + x_lo), y: 4, z: 16, core: 2. Of those that a mesh axis runs over, the one named last changes fastest.
Arguments:
- tokens: bfloat16 [8192, 4096], P('dp', 'test'), may hold values from -6 to 6
- upstream: bfloat16 [8192, 4096], P('dp', 'test'), may hold values from -6 to 6
- rewards: float32 [32, 2], P('dp'), may hold values from -8 to 8
- lengths: int32 [32, 2], P('dp'), may hold values from 1 to 128, as said below
- gate_weight: bfloat16 [4096, 8192], P('dp', 'test'), may hold values from -0.09375 to 0.09375
- up_weight: bfloat16 [4096, 8192], P('dp', 'test'), may hold values from -0.09375 to 0.09375
- down_weight: bfloat16 [8192, 4096], P('test', 'dp'), may hold values from -0.0625 to 0.0625
- in_proj: bfloat16 [4096, 64], replicated, may hold values from -0.09375 to 0.09375
- out_proj: bfloat16 [8192, 64], P('test'), may hold values from -0.0625 to 0.0625
- test_grads: bfloat16 [1024, 4096], P('test'), may hold values from -0.0234375 to 0.0234375
Outputs:
- scores: float32 [32, 1024], P('dp', 'test')
The draws below stay inside these ranges and needn't reach their ends.
Inputs may be any that keep to these rules, and one draw needn't show every extreme that they name: The first lengths[p, s] of the 128 slots of a sequence hold tokens, the rest are padding; shorter sequences are more common, and some sequence fills all 128 slots.
All inputs are finite; a program needn't handle non-finite values.
Results may differ from the reference program's by a relative error of at most 0.0041.
Values may be sent and summed in bfloat16 or wider, within the bound.
No kernel may reach another device: no remote copies, remote signals or barrier semaphores. Data moves between devices by JAX's collectives and lax.ppermute only.
A program may use at most 64 MiB of HBM per device.

```python
import jax
import jax.numpy as jnp
from jax import lax

D = 4096
FF_WIN = 8192
RANK = 64
LMAX = 128
PAIRS = 32
TESTS = 1024
TOKENS = 8192


def draw_lengths(key, part):
    key = jax.random.fold_in(key, 7)
    key_one, key_two, key_three = jax.random.split(key, 3)
    draw_one = jax.random.randint(key_one, (PAIRS * 2,), 1, LMAX + 1)
    draw_two = jax.random.randint(key_two, (PAIRS * 2,), 1, LMAX + 1)
    shorter_len = jnp.minimum(draw_one, draw_two)
    chosen_slot = jax.random.randint(key_three, (), 0, PAIRS * 2)
    filled = jnp.where(jnp.arange(PAIRS * 2) == chosen_slot, LMAX, shorter_len)
    return filled.reshape(PAIRS, 2).astype(jnp.int32)


def shard_levels(key, shape, shards, low, high):
    level, own = 1.0, jax.random.fold_in(key, 6)
    for dim, parts in shards:
        heights = jnp.exp(jax.random.uniform(jax.random.fold_in(own, dim), (parts,), jnp.float32, low / len(shards), high / len(shards)))
        level = level * jnp.repeat(heights, shape[dim] // parts).reshape([-1 if axis == dim else 1 for axis in range(len(shape))])
    return level


def centred(rng, extent, spread, bound, cuts=(), dtype=jnp.bfloat16):
    drawn = spread * jax.random.normal(rng, extent, jnp.float32)
    if cuts:
        drawn = drawn * shard_levels(rng, extent, cuts, -0.22, 0.18)
    return jnp.clip(drawn, -bound, bound).astype(dtype)


def setup_inputs(seed: int = 0) -> dict:
    key_list = jax.random.split(jax.random.key(seed), 11)
    tokens = centred(key_list[0], (TOKENS, D), 1.0, 6.0, ((0, 32), (1, 16)))
    upstream = centred(key_list[1], (TOKENS, D), 1.0, 6.0, ((0, 32), (1, 16)))
    rewards = centred(key_list[2], (PAIRS, 2), 2.0, 8.0, ((0, 32),), jnp.float32)
    lengths = draw_lengths(jax.random.fold_in(key_list[10], 71), 0)
    gate_weight = centred(key_list[4], (D, FF_WIN), D ** -0.5, 0.09375, ((0, 32), (1, 16)))
    up_weight = centred(key_list[5], (D, FF_WIN), D ** -0.5, 0.09375, ((0, 32), (1, 16)))
    down_weight = centred(key_list[6], (FF_WIN, D), FF_WIN ** -0.5, 0.0625, ((0, 16), (1, 32)))
    in_proj = centred(key_list[7], (D, RANK), D ** -0.5, 0.09375)
    out_proj = centred(key_list[8], (FF_WIN, RANK), FF_WIN ** -0.5, 0.0625, ((0, 16),))
    test_grads = centred(key_list[9], (TESTS, RANK * RANK), (RANK * RANK * 16) ** -0.5, 0.0234375, ((0, 16),))
    return dict(tokens=tokens, upstream=upstream, rewards=rewards, lengths=lengths, gate_weight=gate_weight, up_weight=up_weight, down_weight=down_weight, in_proj=in_proj, out_proj=out_proj, test_grads=test_grads)


def silu_slope(gate_pre):
    sigmoid_val = jax.nn.sigmoid(gate_pre)
    return sigmoid_val * (1.0 + gate_pre * (1.0 - sigmoid_val))


def reference(tokens, upstream, rewards, lengths, gate_weight, up_weight, down_weight, in_proj, out_proj, test_grads):
    pair_count = lengths.shape[0]
    width = tokens.shape[1]
    slot_count = tokens.shape[0] // (2 * pair_count)
    pair_coef = jax.nn.sigmoid(rewards[:, 1] - rewards[:, 0])
    gate_wide = gate_weight.astype(jnp.float32)
    up_wide = up_weight.astype(jnp.float32)
    down_wide = down_weight.astype(jnp.float32)
    in_wide = in_proj.astype(jnp.float32)
    out_wide = out_proj.astype(jnp.float32)
    highest = lax.Precision.HIGHEST

    def one_pair(inputs):
        rows_x, rows_dy, length_pair, coef_one = inputs
        rows_x = rows_x.astype(jnp.float32)
        rows_dy = rows_dy.astype(jnp.float32)
        position = lax.broadcasted_iota(jnp.int32, (2, slot_count), 1)
        side_index = lax.broadcasted_iota(jnp.int32, (2, slot_count), 0)
        live_mask = (position < length_pair[:, None]).astype(jnp.float32)
        side_sign = jnp.where(side_index == 1, 1.0, -1.0).astype(jnp.float32)
        row_scale = (coef_one * side_sign * live_mask).reshape(2 * slot_count, 1)
        gate_pre = jnp.dot(rows_x, gate_wide, precision=highest)
        up_pre = jnp.dot(rows_x, up_wide, precision=highest)
        back_grad = jnp.dot(rows_dy, down_wide.T, precision=highest)
        gate_grad = (row_scale * back_grad * up_pre * silu_slope(gate_pre)).astype(jnp.bfloat16)
        in_factor = jnp.dot(rows_x, in_wide, precision=highest)
        out_factor = jnp.dot(gate_grad.astype(jnp.float32), out_wide, precision=highest)
        return jnp.dot(in_factor.T, out_factor, precision=highest)

    pair_grads = lax.map(one_pair, (tokens.reshape(pair_count, 2 * slot_count, width),
                                    upstream.reshape(pair_count, 2 * slot_count, width),
                                    lengths, pair_coef))
    flat_grads = pair_grads.reshape(pair_count, -1).astype(jnp.bfloat16)
    return jnp.dot(flat_grads.astype(jnp.float32), test_grads.astype(jnp.float32).T, precision=highest)
```

```python
import jax
import jax.numpy as jnp
from jax import lax
from jax.experimental import pallas as pl
from jax.experimental.pallas import tpu as pltpu
from jax.sharding import Mesh
from jax.sharding import PartitionSpec as P

SIZES = (2, 16, 4, 2, 2)
NAMES = ("xh", "z", "y", "xl", "c")
DP = ("xh", "z")
TEST = ("y", "xl", "c")
PLANE = ("xh", "y", "xl")
F32 = jnp.float32
BF16 = jnp.bfloat16


def layer_kernel(core_ref, own_ref, other_ref, weight_ref, in_ref, scale_ref, out_ref, pair_ref, pre, back, infac):
    step = pl.program_id(0)
    core = core_ref[0]

    @pl.when(step == 0)
    def _():
        pre[...] = jnp.zeros_like(pre)
        back[...] = jnp.zeros_like(back)
        infac[...] = jnp.zeros_like(infac)

    for pair in range(2):
        rows = slice(pair * 256, pair * 256 + 256)
        for ref, which in ((own_ref, core), (other_ref, 1 - core)):
            base = pl.multiple_of(which * 512, 512)

            def columns(kind):
                return jnp.concatenate(
                    [
                        ref[pair * 2 + half, 0, kind * 256 : kind * 256 + 256, odd * 128 : odd * 128 + 128]
                        for odd in range(2)
                        for half in range(2)
                    ],
                    axis=1,
                )

            features = columns(0)
            pre[rows, :] += jnp.dot(features, weight_ref[pl.ds(base, 512), :512], preferred_element_type=F32)
            infac[rows, :] += jnp.dot(features, in_ref[pl.ds(base, 512), :], preferred_element_type=F32)
            back[rows, :] += jnp.dot(columns(1), weight_ref[pl.ds(base, 512), 512:], preferred_element_type=F32)

    @pl.when(step == pl.num_programs(0) - 1)
    def _():
        gate = pre[:, :256]
        sig = jax.nn.sigmoid(gate)
        slope = sig * (1.0 + gate * (1.0 - sig))
        grad = (scale_ref[:, :1] * back[...] * pre[:, 256:] * slope).astype(BF16)
        out = jnp.dot(grad, out_ref[...], preferred_element_type=F32)
        lane = lax.broadcasted_iota(jnp.int32, (32, 128), 1)
        for pair in range(2):
            rows = slice(pair * 256, pair * 256 + 256)
            mat = lax.dot_general(
                infac[rows, :], out[rows, :], (((0,), (0,)), ((), ())),
                precision=lax.Precision.HIGHEST, preferred_element_type=F32,
            )
            pair_ref[pair] = jnp.where(lane < 64, mat[:32], mat[32:64])


def layer(core, own, other, weights, in_rows, scale, out_twice):
    return pl.pallas_call(
        layer_kernel,
        grid_spec=pltpu.PrefetchScalarGridSpec(
            num_scalar_prefetch=1,
            grid=(4,),
            in_specs=[
                pl.BlockSpec((4, 1, 512, 256), lambda q, c: (0, q, 0, 0)),
                pl.BlockSpec((4, 1, 512, 256), lambda q, c: (0, q, 0, 0)),
                pl.BlockSpec((1024, 768), lambda q, c: (q, 0)),
                pl.BlockSpec((1024, 64), lambda q, c: (q, 0)),
                pl.BlockSpec((512, 128), lambda q, c: (0, 0)),
                pl.BlockSpec((256, 128), lambda q, c: (0, 0)),
            ],
            out_specs=pl.BlockSpec((2, 32, 128), lambda q, c: (0, 0, 0)),
            scratch_shapes=[
                pltpu.VMEM((512, 512), F32),
                pltpu.VMEM((512, 256), F32),
                pltpu.VMEM((512, 64), F32),
            ],
        ),
        out_shape=jax.ShapeDtypeStruct((2, 32, 128), F32),
        compiler_params=pltpu.CompilerParams(vmem_limit_bytes=40 * 1024 * 1024),
        cost_estimate=pl.CostEstimate(flops=2 * 512 * 4096 * 832, bytes_accessed=15 * 1024 * 1024, transcendentals=131072),
    )(core, own, other, weights, in_rows, scale, out_twice)


def per_device(
    tokens, upstream, rewards, lengths, gate_weight, up_weight, down_weight, in_proj, out_proj, test_grads
):
    xh = lax.axis_index("xh")
    core = lax.axis_index("c")
    swap = [(0, 1), (1, 0)]

    halves = [
        jnp.concatenate(
            [gate_weight[:, lo : lo + 256], up_weight[:, lo : lo + 256], down_weight[lo : lo + 256].T], axis=1
        )
        for lo in (0, 256)
    ]
    mine = jnp.where(xh == 0, halves[0], halves[1])
    theirs = lax.ppermute(jnp.where(xh == 0, halves[1], halves[0]), "xh", swap)
    block = jnp.where(xh == 0, jnp.stack([mine, theirs]), jnp.stack([theirs, mine]))
    weights = lax.all_gather(block, "z").reshape(4096, 768)

    nothing = theirs[:1, :256] * 0
    acts = jnp.concatenate([tokens, upstream], axis=0) + nothing
    own = lax.all_to_all(jnp.broadcast_to(acts[None], (16, 512, 256)), PLANE, 0, 0)
    other = lax.ppermute(own, "c", swap)

    position = lax.broadcasted_iota(jnp.int32, (2, 128), 1)
    side = lax.broadcasted_iota(jnp.int32, (2, 128), 0)
    coef = jax.nn.sigmoid(rewards[0, 1] - rewards[0, 0])
    live = (position < lengths.reshape(2, 1)).astype(F32)
    scale = (coef * jnp.where(side == 1, 1.0, -1.0).astype(F32) * live).reshape(2, 128)
    scale_other = lax.ppermute(scale, "xh", swap)
    scale = jnp.where(xh == 0, jnp.stack([scale, scale_other]), jnp.stack([scale_other, scale]))
    scale = jnp.broadcast_to(scale.reshape(512, 1), (512, 128))

    in_rows = in_proj.reshape(2, 16, 128, 32, 2).transpose(1, 0, 2, 4, 3).reshape(4096, 64)
    out_half = jnp.where(xh == 0, out_proj[:256], out_proj[256:])
    out_twice = jnp.concatenate([out_half, out_half], axis=1)

    pairs = layer(
        core.reshape(1).astype(jnp.int32),
        own.reshape(4, 4, 512, 256),
        other.reshape(4, 4, 512, 256),
        weights,
        in_rows,
        scale,
        out_twice,
    )
    spread = jnp.broadcast_to(pairs[:, None], (2, 16, 32, 128)).reshape(32, 32, 128)
    parts = lax.all_to_all(spread, ("xh",) + TEST, 0, 0)
    flat = jnp.sum(parts, axis=0).astype(BF16).reshape(1, 4096)
    return lax.dot_general(flat, test_grads, (((1,), (1,)), ((), ())), preferred_element_type=F32)


def solution(mesh):
    fine = Mesh(mesh.devices.reshape(SIZES), NAMES)
    placed = (
        P(DP, TEST),
        P(DP, TEST),
        P(DP, None),
        P(DP, None),
        P(DP, TEST),
        P(DP, TEST),
        P(TEST, DP),
        P(),
        P(TEST, None),
        P(TEST, None),
    )
    return jax.shard_map(per_device, mesh=fine, in_specs=placed, out_specs=P(DP, TEST), check_vma=False)
```

```python
import jax
import jax.numpy as jnp
from jax import lax
from jax.experimental import pallas as pl
from jax.experimental.pallas import tpu as pltpu
from jax.sharding import Mesh
from jax.sharding import PartitionSpec as P

SIZES = (2, 16, 4, 2, 2)
NAMES = ("xh", "z", "y", "xl", "c")
DP = ("xh", "z")
TEST = ("y", "xl", "c")
PLANE = ("xh", "y", "xl")
F32 = jnp.float32
BF16 = jnp.bfloat16
MIB = 1024 * 1024


def pack_kernel(place, gate_ref, up_ref, down_ref, mine_ref, send_ref):
    xh = place[0]
    for half, ref in ((xh, mine_ref), (1 - xh, send_ref)):
        units = pl.ds(pl.multiple_of(half * 256, 256), 256)
        ref[:, :256] = gate_ref[:, units]
        ref[:, 256:512] = up_ref[:, units]
        ref[:, 512:] = down_ref[units, :].T


def pack(place, gate_weight, up_weight, down_weight):
    here = pl.BlockSpec(memory_space=pltpu.VMEM)
    return pl.pallas_call(
        pack_kernel,
        in_specs=[pl.BlockSpec(memory_space=pltpu.SMEM), here, here, here],
        out_specs=[here, here],
        out_shape=[jax.ShapeDtypeStruct((128, 768), BF16)] * 2,
        compiler_params=pltpu.CompilerParams(vmem_limit_bytes=8 * MIB),
        cost_estimate=pl.CostEstimate(flops=0, bytes_accessed=768 * 1024, transcendentals=0),
    )(place, *(pltpu.with_memory_space_constraint(each, pltpu.HBM) for each in (gate_weight, up_weight, down_weight)))


def order_kernel(place, own_ref, other_ref, in_ref, rows_ref, infac_ref):
    core = place[2]
    infac = jnp.zeros((512, 64), F32)
    for plane in range(16):
        ours = (plane // 2) % 2 == core
        lanes = slice(plane % 2 * 128, plane % 2 * 128 + 128)
        for half in range(2):
            into = slice(plane % 8 * 256 + half * 128, plane % 8 * 256 + half * 128 + 128)
            for pair in range(2):
                for kind in range(2):
                    slots = slice(kind * 256, kind * 256 + 256)
                    rows_ref[plane // 8, kind, pair * 256 : pair * 256 + 256, into] = jnp.where(
                        ours,
                        own_ref[pair, half, plane // 4, slots, lanes],
                        other_ref[pair, half, plane // 4, slots, lanes],
                    )
        in_rows = jnp.concatenate(
            [in_ref[(half * 16 + plane) * 128 : (half * 16 + plane) * 128 + 128, :] for half in range(2)], axis=0
        )
        infac += jnp.dot(
            rows_ref[plane // 8, 0, :, plane % 8 * 256 : plane % 8 * 256 + 256], in_rows, preferred_element_type=F32
        )
    row = lax.broadcasted_iota(jnp.int32, (64, 64), 0)
    column = lax.broadcasted_iota(jnp.int32, (64, 64), 1)
    even_first = (row == jnp.where(column < 32, 2 * column, 2 * column - 63)).astype(F32)
    infac_ref[...] = jnp.dot(infac, even_first, precision=lax.Precision.HIGHEST, preferred_element_type=F32)


def order(place, own, other, in_proj):
    here = pl.BlockSpec(memory_space=pltpu.VMEM)
    return pl.pallas_call(
        order_kernel,
        in_specs=[pl.BlockSpec(memory_space=pltpu.SMEM), here, here, here],
        out_specs=[here, here],
        out_shape=[jax.ShapeDtypeStruct((2, 2, 512, 2048), BF16), jax.ShapeDtypeStruct((512, 64), F32)],
        compiler_params=pltpu.CompilerParams(vmem_limit_bytes=24 * MIB),
        cost_estimate=pl.CostEstimate(flops=2 * 512 * 4096 * 64, bytes_accessed=17 * MIB, transcendentals=0),
    )(place, own, other, in_proj)


def layer_kernel(rows_ref, weight_ref, infac_ref, scale_ref, out_ref, pair_ref, pre, back):
    step = pl.program_id(0)
    one = jnp.dot(rows_ref[0, 0], weight_ref[:, :512], preferred_element_type=F32)
    two = jnp.dot(rows_ref[0, 1], weight_ref[:, 512:], preferred_element_type=F32)

    @pl.when(step == 0)
    def _():
        pre[...] = one
        back[...] = two

    @pl.when(step > 0)
    def _():
        pre[...] += one
        back[...] += two

    @pl.when(step == pl.num_programs(0) - 1)
    def _():
        gate = pre[:, :256]
        sig = jax.nn.sigmoid(gate)
        slope = sig * (1.0 + gate * (1.0 - sig))
        grad = (scale_ref[:, :1] * back[...] * pre[:, 256:] * slope).astype(BF16)
        out = jnp.dot(grad, out_ref[...], preferred_element_type=F32)
        lane = lax.broadcasted_iota(jnp.int32, (32, 128), 1)
        for pair in range(2):
            slots = slice(pair * 256, pair * 256 + 256)
            mat = lax.dot_general(
                infac_ref[slots, :], out[slots, :], (((0,), (0,)), ((), ())),
                precision=lax.Precision.HIGHEST, preferred_element_type=F32,
            )
            pair_ref[pair] = jnp.where(lane < 64, mat[:32], mat[32:64]).astype(BF16)


def layer(rows, weights, infac, scale, out_twice):
    here = pl.BlockSpec(memory_space=pltpu.VMEM)
    rows = pltpu.with_memory_space_constraint(rows, pltpu.HBM)
    weights = pltpu.with_memory_space_constraint(weights, pltpu.HBM)
    return pl.pallas_call(
        layer_kernel,
        grid=(2,),
        in_specs=[
            pl.BlockSpec((1, 2, 512, 2048), lambda q: (q, 0, 0, 0)),
            pl.BlockSpec((2048, 768), lambda q: (q, 0)),
            here,
            here,
            here,
        ],
        out_specs=pl.BlockSpec((2, 32, 128), lambda q: (0, 0, 0)),
        out_shape=jax.ShapeDtypeStruct((2, 32, 128), BF16),
        scratch_shapes=[pltpu.VMEM((512, 512), F32), pltpu.VMEM((512, 256), F32)],
        compiler_params=pltpu.CompilerParams(vmem_limit_bytes=40 * MIB),
        cost_estimate=pl.CostEstimate(flops=2 * 512 * 4096 * 768, bytes_accessed=15 * MIB, transcendentals=131072),
    )(rows, weights, infac, scale, out_twice)


def per_device(
    tokens, upstream, rewards, lengths, gate_weight, up_weight, down_weight, in_proj, out_proj, test_grads
):
    xh, z, core = lax.axis_index("xh"), lax.axis_index("z"), lax.axis_index("c")
    place = jnp.stack([xh, z, core]).astype(jnp.int32)
    swap = [(0, 1), (1, 0)]

    mine, send = pack(place, gate_weight, up_weight, down_weight)
    theirs = lax.ppermute(send, "xh", swap)
    block = jnp.where(xh == 0, jnp.stack([mine, theirs]), jnp.stack([theirs, mine]))
    weights = lax.all_gather(block, "z").reshape(4096, 768)

    acts = jnp.concatenate([tokens, upstream], axis=0) + theirs[0, 0] * 0
    own = lax.all_to_all(jnp.broadcast_to(acts[None], (16, 512, 256)), PLANE, 0, 0).reshape(2, 2, 4, 512, 256)
    other = lax.ppermute(own, "c", swap)

    position = lax.broadcasted_iota(jnp.int32, (2, 128), 1)
    side = lax.broadcasted_iota(jnp.int32, (2, 128), 0)
    coef = jax.nn.sigmoid(rewards[0, 1] - rewards[0, 0])
    live = (position < lengths.reshape(2, 1)).astype(F32)
    scale = (coef * jnp.where(side == 1, 1.0, -1.0).astype(F32) * live).reshape(2, 128)
    scale_other = lax.ppermute(scale, "xh", swap)
    scale = jnp.where(xh == 0, jnp.stack([scale, scale_other]), jnp.stack([scale_other, scale]))
    scale = jnp.broadcast_to(scale.reshape(512, 1), (512, 128))

    out_half = jnp.where(xh == 0, out_proj[:256], out_proj[256:])
    out_twice = jnp.concatenate([out_half, out_half], axis=1)

    rows, infac = order(place, own, other, in_proj)
    pairs = layer(rows, weights, infac, scale, out_twice)
    spread = jnp.broadcast_to(pairs[:, None], (2, 16, 32, 128)).reshape(32, 32, 128)
    parts = lax.all_to_all(spread, ("xh",) + TEST, 0, 0)
    flat = jnp.sum(parts.astype(F32), axis=0).astype(BF16).reshape(1, 4096)
    return lax.dot_general(flat, test_grads, (((1,), (1,)), ((), ())), preferred_element_type=F32)


def solution(mesh):
    fine = Mesh(mesh.devices.reshape(SIZES), NAMES)
    placed = (
        P(DP, TEST),
        P(DP, TEST),
        P(DP, None),
        P(DP, None),
        P(DP, TEST),
        P(DP, TEST),
        P(TEST, DP),
        P(),
        P(TEST, None),
        P(TEST, None),
    )
    return jax.shard_map(per_device, mesh=fine, in_specs=placed, out_specs=P(DP, TEST), check_vma=False)
```

```python
import jax
import jax.numpy as jnp
from jax import lax
from jax.experimental import pallas as pl
from jax.experimental.pallas import tpu as pltpu
from jax.sharding import Mesh
from jax.sharding import PartitionSpec as P

SIZES = (2, 16, 4, 2, 2)
NAMES = ("xh", "z", "y", "xl", "c")
DP = ("xh", "z")
TEST = ("y", "xl", "c")
PLANE = ("xh", "y", "xl")
F32 = jnp.float32
BF16 = jnp.bfloat16
MIB = 1024 * 1024
PARTS = 8


def pack(gives, place, gate_weight, up_weight, down_weight):
    def kernel(place, gate_ref, up_ref, down_ref, packed_ref):
        xh = place[0]
        units = pl.ds(pl.multiple_of((1 - xh if gives else xh) * 256, 256), 256)
        slot = packed_ref if gives else packed_ref.at[xh]
        slot[:, :256] = gate_ref[:, units]
        slot[:, 256:512] = up_ref[:, units]
        slot[:, 512:] = down_ref[units, :].T

    here = pl.BlockSpec(memory_space=pltpu.VMEM)
    return pl.pallas_call(
        kernel,
        in_specs=[pl.BlockSpec(memory_space=pltpu.SMEM), here, here, here],
        out_specs=here,
        out_shape=jax.ShapeDtypeStruct((128, 768) if gives else (2, 128, 768), BF16),
        compiler_params=pltpu.CompilerParams(vmem_limit_bytes=8 * MIB),
        cost_estimate=pl.CostEstimate(flops=0, bytes_accessed=768 * 1024, transcendentals=0),
    )(place, *(pltpu.with_memory_space_constraint(each, pltpu.HBM) for each in (gate_weight, up_weight, down_weight)))


def order_kernel(place, own_ref, other_ref, in_ref, rows_ref, infac_ref):
    core = place[2]
    infac = jnp.zeros((512, 64), F32)
    for plane in range(16):
        ours = (plane // 2) % 2 == core
        lanes = slice(plane % 2 * 128, plane % 2 * 128 + 128)
        for half in range(2):
            into = slice(plane % 2 * 256 + half * 128, plane % 2 * 256 + half * 128 + 128)
            for pair in range(2):
                for kind in range(2):
                    slots = slice(kind * 256, kind * 256 + 256)
                    rows_ref[plane // 2, kind, pair * 256 : pair * 256 + 256, into] = jnp.where(
                        ours,
                        own_ref[pair, half, plane // 4, slots, lanes],
                        other_ref[pair, half, plane // 4, slots, lanes],
                    )
        in_rows = jnp.concatenate(
            [in_ref[(half * 16 + plane) * 128 : (half * 16 + plane) * 128 + 128, :] for half in range(2)], axis=0
        )
        infac += jnp.dot(
            rows_ref[plane // 2, 0, :, plane % 2 * 256 : plane % 2 * 256 + 256], in_rows, preferred_element_type=F32
        )
    row = lax.broadcasted_iota(jnp.int32, (64, 64), 0)
    column = lax.broadcasted_iota(jnp.int32, (64, 64), 1)
    even_first = (row == jnp.where(column < 32, 2 * column, 2 * column - 63)).astype(F32)
    infac_ref[...] = jnp.dot(infac, even_first, precision=lax.Precision.HIGHEST, preferred_element_type=F32)


def order(place, own, other, in_proj):
    here = pl.BlockSpec(memory_space=pltpu.VMEM)
    return pl.pallas_call(
        order_kernel,
        in_specs=[pl.BlockSpec(memory_space=pltpu.SMEM), here, here, here],
        out_specs=[here, here],
        out_shape=[jax.ShapeDtypeStruct((PARTS, 2, 512, 512), BF16), jax.ShapeDtypeStruct((512, 64), F32)],
        compiler_params=pltpu.CompilerParams(vmem_limit_bytes=24 * MIB),
        cost_estimate=pl.CostEstimate(flops=2 * 512 * 4096 * 64, bytes_accessed=17 * MIB, transcendentals=0),
    )(place, own, other, in_proj)


def layer_kernel(rows_ref, weight_ref, infac_ref, scale_ref, out_ref, pair_ref, rows, weights, pre, back, sems):
    copies = [
        (
            pltpu.make_async_copy(weight_ref.at[pl.ds(part * 512, 512), :], weights.at[part], sems.at[0, part]),
            pltpu.make_async_copy(rows_ref.at[part], rows.at[part], sems.at[1, part]),
        )
        for part in range(PARTS)
    ]
    for two in copies:
        for copy in two:
            copy.start()
    for part in range(PARTS):
        for copy in copies[part]:
            copy.wait()
        one = jnp.dot(rows[part, 0], weights[part, :, :512], preferred_element_type=F32)
        two = jnp.dot(rows[part, 1], weights[part, :, 512:], preferred_element_type=F32)
        if part:
            pre[...] += one
            back[...] += two
        else:
            pre[...] = one
            back[...] = two
    gate = pre[:, :256]
    sig = jax.nn.sigmoid(gate)
    slope = sig * (1.0 + gate * (1.0 - sig))
    grad = (scale_ref[:, :1] * back[...] * pre[:, 256:] * slope).astype(BF16)
    out = jnp.dot(grad, out_ref[...], preferred_element_type=F32)
    lane = lax.broadcasted_iota(jnp.int32, (32, 128), 1)
    for pair in range(2):
        slots = slice(pair * 256, pair * 256 + 256)
        mat = lax.dot_general(
            infac_ref[slots, :], out[slots, :], (((0,), (0,)), ((), ())),
            precision=lax.Precision.HIGHEST, preferred_element_type=F32,
        )
        pair_ref[pair] = jnp.where(lane < 64, mat[:32], mat[32:64]).astype(BF16)


def layer(rows, weights, infac, scale, out_twice):
    here = pl.BlockSpec(memory_space=pltpu.VMEM)
    there = pl.BlockSpec(memory_space=pl.ANY)
    rows = pltpu.with_memory_space_constraint(rows, pltpu.HBM)
    weights = pltpu.with_memory_space_constraint(weights, pltpu.HBM)
    return pl.pallas_call(
        layer_kernel,
        in_specs=[there, there, here, here, here],
        out_specs=here,
        out_shape=jax.ShapeDtypeStruct((2, 32, 128), BF16),
        scratch_shapes=[
            pltpu.VMEM((PARTS, 2, 512, 512), BF16),
            pltpu.VMEM((PARTS, 512, 768), BF16),
            pltpu.VMEM((512, 512), F32),
            pltpu.VMEM((512, 256), F32),
            pltpu.SemaphoreType.DMA((2, PARTS)),
        ],
        compiler_params=pltpu.CompilerParams(vmem_limit_bytes=40 * MIB),
        cost_estimate=pl.CostEstimate(flops=2 * 512 * 4096 * 768, bytes_accessed=15 * MIB, transcendentals=131072),
    )(rows, weights, infac, scale, out_twice)


def per_device(
    tokens, upstream, rewards, lengths, gate_weight, up_weight, down_weight, in_proj, out_proj, test_grads
):
    xh, z, core = lax.axis_index("xh"), lax.axis_index("z"), lax.axis_index("c")
    place = jnp.stack([xh, z, core]).astype(jnp.int32)
    swap = [(0, 1), (1, 0)]

    theirs = lax.ppermute(pack(True, place, gate_weight, up_weight, down_weight), "xh", swap)
    mine = pack(False, place, gate_weight, up_weight, down_weight)
    block = lax.dynamic_update_slice(mine, theirs[None], (1 - xh, 0, 0))
    weights = lax.all_gather(block, "z").reshape(4096, 768)

    acts = jnp.concatenate([tokens, upstream], axis=0) + theirs[0, 0] * 0
    own = lax.all_to_all(jnp.broadcast_to(acts[None], (16, 512, 256)), PLANE, 0, 0).reshape(2, 2, 4, 512, 256)
    other = lax.ppermute(own, "c", swap)

    position = lax.broadcasted_iota(jnp.int32, (2, 128), 1)
    side = lax.broadcasted_iota(jnp.int32, (2, 128), 0)
    coef = jax.nn.sigmoid(rewards[0, 1] - rewards[0, 0])
    live = (position < lengths.reshape(2, 1)).astype(F32)
    scale = (coef * jnp.where(side == 1, 1.0, -1.0).astype(F32) * live).reshape(2, 128)
    scale_other = lax.ppermute(scale, "xh", swap)
    scale = jnp.where(xh == 0, jnp.stack([scale, scale_other]), jnp.stack([scale_other, scale]))
    scale = jnp.broadcast_to(scale.reshape(512, 1), (512, 128))

    out_half = jnp.where(xh == 0, out_proj[:256], out_proj[256:])
    out_twice = jnp.concatenate([out_half, out_half], axis=1)

    rows, infac = order(place, own, other, in_proj)
    pairs = layer(rows, weights, infac, scale, out_twice)
    spread = jnp.broadcast_to(pairs[:, None], (2, 16, 32, 128)).reshape(32, 32, 128)
    parts = lax.all_to_all(spread, ("xh",) + TEST, 0, 0)
    flat = jnp.sum(parts.astype(F32), axis=0).astype(BF16).reshape(1, 4096)
    return lax.dot_general(flat, test_grads, (((1,), (1,)), ((), ())), preferred_element_type=F32)


def solution(mesh):
    fine = Mesh(mesh.devices.reshape(SIZES), NAMES)
    placed = (
        P(DP, TEST),
        P(DP, TEST),
        P(DP, None),
        P(DP, None),
        P(DP, TEST),
        P(DP, TEST),
        P(TEST, DP),
        P(),
        P(TEST, None),
        P(TEST, None),
    )
    return jax.shard_map(per_device, mesh=fine, in_specs=placed, out_specs=P(DP, TEST), check_vma=False)
```

```python
import jax
import jax.numpy as jnp
from jax import lax
from jax.experimental import pallas as pl
from jax.experimental.pallas import tpu as pltpu
from jax.sharding import Mesh
from jax.sharding import PartitionSpec as P

SIZES = (2, 16, 4, 2, 2)
NAMES = ("xh", "z", "y", "xl", "c")
DP = ("xh", "z")
TEST = ("y", "xl", "c")
PLANE = ("xh", "y", "xl")
F32 = jnp.float32
BF16 = jnp.bfloat16
MIB = 1024 * 1024
PARTS = 8


def pack(gives, place, gate_weight, up_weight, down_weight):
    def kernel(place, gate_ref, up_ref, down_ref, packed_ref):
        xh = place[0]
        units = pl.ds(pl.multiple_of((1 - xh if gives else xh) * 256, 256), 256)
        slot = packed_ref if gives else packed_ref.at[xh]
        slot[:, :256] = gate_ref[:, units]
        slot[:, 256:512] = up_ref[:, units]
        slot[:, 512:] = down_ref[units, :].T

    here = pl.BlockSpec(memory_space=pltpu.VMEM)
    return pl.pallas_call(
        kernel,
        in_specs=[pl.BlockSpec(memory_space=pltpu.SMEM), here, here, here],
        out_specs=here,
        out_shape=jax.ShapeDtypeStruct((128, 768) if gives else (2, 128, 768), BF16),
        compiler_params=pltpu.CompilerParams(vmem_limit_bytes=8 * MIB),
        cost_estimate=pl.CostEstimate(flops=0, bytes_accessed=768 * 1024, transcendentals=0),
    )(place, *(pltpu.with_memory_space_constraint(each, pltpu.HBM) for each in (gate_weight, up_weight, down_weight)))


def live_blocks(place):
    counts = [(place[3 + n] + 15) // 16 for n in range(4)]
    starts = [jnp.int32(0)]
    for count in counts:
        starts.append(starts[-1] + count)
    return counts, starts


def order_kernel(place, own_ref, other_ref, in_ref, scale_ref, rows_ref, infac_ref, packed_ref):
    core = place[2]
    counts, starts = live_blocks(place)
    for sequence in range(4):
        pair, side = sequence // 2, sequence % 2

        def move(n, carry):
            source = pl.multiple_of(side * 128 + n * 16, 16)
            target = pl.ds(pl.multiple_of((starts[sequence] + n) * 16, 16), 16)
            for plane in range(16):
                ours = (plane // 2) % 2 == core
                lanes = slice(plane % 2 * 128, plane % 2 * 128 + 128)
                for half in range(2):
                    into = slice(plane % 2 * 256 + half * 128, plane % 2 * 256 + half * 128 + 128)
                    for kind in range(2):
                        slots = pl.ds(pl.multiple_of(kind * 256 + source, 16), 16)
                        rows_ref[plane // 2, kind, target, into] = jnp.where(
                            ours,
                            own_ref[pair, half, plane // 4, slots, lanes],
                            other_ref[pair, half, plane // 4, slots, lanes],
                        )
            packed_ref[target, :] = scale_ref[pl.ds(pl.multiple_of(pair * 256 + source, 16), 16), :]
            return carry

        lax.fori_loop(0, counts[sequence], move, 0)

    def clear(n, carry):
        target = pl.ds(pl.multiple_of(n * 16, 16), 16)
        for part in range(PARTS):
            for kind in range(2):
                rows_ref[part, kind, target, :] = jnp.zeros((16, 512), BF16)
        packed_ref[target, :] = jnp.zeros((16, 128), F32)
        return carry

    lax.fori_loop(starts[4], jnp.where(starts[4] > 16, 32, 16), clear, 0)

    infac = jnp.zeros((512, 64), F32)
    for plane in range(16):
        in_rows = jnp.concatenate(
            [in_ref[(half * 16 + plane) * 128 : (half * 16 + plane) * 128 + 128, :] for half in range(2)], axis=0
        )
        infac += jnp.dot(
            rows_ref[plane // 2, 0, :, plane % 2 * 256 : plane % 2 * 256 + 256], in_rows, preferred_element_type=F32
        )
    row = lax.broadcasted_iota(jnp.int32, (64, 64), 0)
    column = lax.broadcasted_iota(jnp.int32, (64, 64), 1)
    even_first = (row == jnp.where(column < 32, 2 * column, 2 * column - 63)).astype(F32)
    infac = jnp.dot(infac, even_first, precision=lax.Precision.HIGHEST, preferred_element_type=F32)
    first = lax.broadcasted_iota(jnp.int32, (512, 64), 0) < starts[2] * 16
    infac_ref[...] = jnp.concatenate([jnp.where(first, infac, 0.0), jnp.where(first, 0.0, infac)], axis=1)


def order(place, own, other, in_proj, scale):
    here = pl.BlockSpec(memory_space=pltpu.VMEM)
    return pl.pallas_call(
        order_kernel,
        in_specs=[pl.BlockSpec(memory_space=pltpu.SMEM), here, here, here, here],
        out_specs=[here, here, here],
        out_shape=[
            jax.ShapeDtypeStruct((PARTS, 2, 512, 512), BF16),
            jax.ShapeDtypeStruct((512, 128), F32),
            jax.ShapeDtypeStruct((512, 128), F32),
        ],
        compiler_params=pltpu.CompilerParams(vmem_limit_bytes=24 * MIB),
        cost_estimate=pl.CostEstimate(flops=2 * 512 * 4096 * 64, bytes_accessed=17 * MIB, transcendentals=0),
    )(place, own, other, in_proj, scale)


def layer_kernel(
    place, rows_ref, weight_ref, infac_ref, scale_ref, out_ref, pair_ref, rows, weights, pre, back, sems
):
    def run(count):
        some = slice(0, count)
        copies = [
            (
                pltpu.make_async_copy(weight_ref.at[pl.ds(part * 512, 512), :], weights.at[part], sems.at[0, part]),
                pltpu.make_async_copy(rows_ref.at[part, :, some, :], rows.at[part, :, some, :], sems.at[1, part]),
            )
            for part in range(PARTS)
        ]
        for both in copies:
            for copy in both:
                copy.start()
        for part in range(PARTS):
            for copy in copies[part]:
                copy.wait()
            one = jnp.dot(rows[part, 0, some], weights[part, :, :512], preferred_element_type=F32)
            two = jnp.dot(rows[part, 1, some], weights[part, :, 512:], preferred_element_type=F32)
            if part:
                pre[some, :] += one
                back[some, :] += two
            else:
                pre[some, :] = one
                back[some, :] = two
        gate = pre[some, :256]
        sig = jax.nn.sigmoid(gate)
        slope = sig * (1.0 + gate * (1.0 - sig))
        grad = (scale_ref[some, :1] * back[some, :] * pre[some, 256:] * slope).astype(BF16)
        out = jnp.dot(grad, out_ref[...], preferred_element_type=F32)
        mats = lax.dot_general(
            infac_ref[some, :], out, (((0,), (0,)), ((), ())),
            precision=lax.Precision.HIGHEST, preferred_element_type=F32,
        )
        lane = lax.broadcasted_iota(jnp.int32, (32, 128), 1)
        for pair in range(2):
            mat = mats[pair * 64 : pair * 64 + 64]
            pair_ref[pair] = jnp.where(lane < 64, mat[:32], mat[32:]).astype(BF16)

    few = live_blocks(place)[1][4] <= 16
    pl.when(few)(lambda: run(256))
    pl.when(jnp.logical_not(few))(lambda: run(512))


def layer(place, rows, weights, infac, scale, out_twice):
    here = pl.BlockSpec(memory_space=pltpu.VMEM)
    there = pl.BlockSpec(memory_space=pl.ANY)
    rows = pltpu.with_memory_space_constraint(rows, pltpu.HBM)
    weights = pltpu.with_memory_space_constraint(weights, pltpu.HBM)
    return pl.pallas_call(
        layer_kernel,
        in_specs=[pl.BlockSpec(memory_space=pltpu.SMEM), there, there, here, here, here],
        out_specs=here,
        out_shape=jax.ShapeDtypeStruct((2, 32, 128), BF16),
        scratch_shapes=[
            pltpu.VMEM((PARTS, 2, 512, 512), BF16),
            pltpu.VMEM((PARTS, 512, 768), BF16),
            pltpu.VMEM((512, 512), F32),
            pltpu.VMEM((512, 256), F32),
            pltpu.SemaphoreType.DMA((2, PARTS)),
        ],
        compiler_params=pltpu.CompilerParams(vmem_limit_bytes=40 * MIB),
        cost_estimate=pl.CostEstimate(flops=2 * 512 * 4096 * 768, bytes_accessed=15 * MIB, transcendentals=131072),
    )(place, rows, weights, infac, scale, out_twice)


def per_device(
    tokens, upstream, rewards, lengths, gate_weight, up_weight, down_weight, in_proj, out_proj, test_grads
):
    xh, z, core = lax.axis_index("xh"), lax.axis_index("z"), lax.axis_index("c")
    place = jnp.stack([xh, z, core]).astype(jnp.int32)
    swap = [(0, 1), (1, 0)]

    theirs = lax.ppermute(pack(True, place, gate_weight, up_weight, down_weight), "xh", swap)
    mine = pack(False, place, gate_weight, up_weight, down_weight)
    block = lax.dynamic_update_slice(mine, theirs[None], (1 - xh, 0, 0))
    weights = lax.all_gather(block, "z").reshape(4096, 768)

    acts = jnp.concatenate([tokens, upstream], axis=0) + theirs[0, 0] * 0
    own = lax.all_to_all(jnp.broadcast_to(acts[None], (16, 512, 256)), PLANE, 0, 0).reshape(2, 2, 4, 512, 256)
    other = lax.ppermute(own, "c", swap)

    coef = jax.nn.sigmoid(rewards[0, 1] - rewards[0, 0])
    known = jnp.pad(jnp.stack([coef, lengths[0, 0].astype(F32), lengths[0, 1].astype(F32)]), (0, 125))[None]
    known_other = lax.ppermute(known, "xh", swap)
    known = jnp.where(xh == 0, jnp.concatenate([known, known_other]), jnp.concatenate([known_other, known]))
    position = lax.broadcasted_iota(jnp.int32, (2, 2, 128), 2).astype(F32)
    side = lax.broadcasted_iota(jnp.int32, (2, 2, 128), 1)
    live = (position < known[:, 1:3, None]).astype(F32)
    scale = known[:, :1, None] * jnp.where(side == 1, 1.0, -1.0).astype(F32) * live
    scale = jnp.broadcast_to(scale.reshape(512, 1), (512, 128))
    ready = jnp.concatenate([place, known[:, 1:3].reshape(4).astype(jnp.int32)])

    out_half = jnp.where(xh == 0, out_proj[:256], out_proj[256:])
    out_twice = jnp.concatenate([out_half, out_half], axis=1)

    rows, infac, packed = order(ready, own, other, in_proj, scale)
    pairs = layer(ready, rows, weights, infac, packed, out_twice)
    spread = jnp.broadcast_to(pairs[:, None], (2, 16, 32, 128)).reshape(32, 32, 128)
    parts = lax.all_to_all(spread, ("xh",) + TEST, 0, 0)
    flat = jnp.sum(parts.astype(F32), axis=0).astype(BF16).reshape(1, 4096)
    return lax.dot_general(flat, test_grads, (((1,), (1,)), ((), ())), preferred_element_type=F32)


def solution(mesh):
    fine = Mesh(mesh.devices.reshape(SIZES), NAMES)
    placed = (
        P(DP, TEST),
        P(DP, TEST),
        P(DP, None),
        P(DP, None),
        P(DP, TEST),
        P(DP, TEST),
        P(TEST, DP),
        P(),
        P(TEST, None),
        P(TEST, None),
    )
    return jax.shard_map(per_device, mesh=fine, in_specs=placed, out_specs=P(DP, TEST), check_vma=False)
```

```python
import jax
import jax.numpy as jnp
from jax import lax
from jax.experimental import pallas as pl
from jax.experimental.pallas import tpu as pltpu
from jax.sharding import Mesh
from jax.sharding import PartitionSpec as P

SIZES = (2, 16, 4, 2, 2)
NAMES = ("xh", "z", "y", "xl", "c")
DP = ("xh", "z")
TEST = ("y", "xl", "c")
PLANE = ("xh", "y", "xl")
F32 = jnp.float32
BF16 = jnp.bfloat16
MIB = 1024 * 1024
PARTS = 8
STEPS = (192, 288, 384, 512)


def pack(gives, place, gate_weight, up_weight, down_weight):
    def kernel(place, gate_ref, up_ref, down_ref, packed_ref):
        xh = place[0]
        units = pl.ds(pl.multiple_of((1 - xh if gives else xh) * 256, 256), 256)
        slot = packed_ref if gives else packed_ref.at[xh]
        slot[:, :256] = gate_ref[:, units]
        slot[:, 256:512] = up_ref[:, units]
        slot[:, 512:] = down_ref[units, :].T

    here = pl.BlockSpec(memory_space=pltpu.VMEM)
    return pl.pallas_call(
        kernel,
        in_specs=[pl.BlockSpec(memory_space=pltpu.SMEM), here, here, here],
        out_specs=here,
        out_shape=jax.ShapeDtypeStruct((128, 768) if gives else (2, 128, 768), BF16),
        compiler_params=pltpu.CompilerParams(vmem_limit_bytes=8 * MIB),
        cost_estimate=pl.CostEstimate(flops=0, bytes_accessed=768 * 1024, transcendentals=0),
    )(place, *(pltpu.with_memory_space_constraint(each, pltpu.HBM) for each in (gate_weight, up_weight, down_weight)))


def live_blocks(place):
    counts = [(place[3 + n] + 15) // 16 for n in range(4)]
    starts = [jnp.int32(0)]
    for count in counts:
        starts.append(starts[-1] + count)
    return counts, starts


def order_kernel(place, own_ref, other_ref, in_ref, scale_ref, rows_ref, infac_ref, packed_ref):
    core = place[2]
    counts, starts = live_blocks(place)
    for sequence in range(4):
        pair, side = sequence // 2, sequence % 2

        def move(n, carry):
            source = pl.multiple_of(side * 128 + n * 16, 16)
            target = pl.ds(pl.multiple_of((starts[sequence] + n) * 16, 16), 16)
            for plane in range(16):
                ours = (plane // 2) % 2 == core
                lanes = slice(plane % 2 * 128, plane % 2 * 128 + 128)
                for half in range(2):
                    into = slice(plane % 2 * 256 + half * 128, plane % 2 * 256 + half * 128 + 128)
                    for kind in range(2):
                        slots = pl.ds(pl.multiple_of(kind * 256 + source, 16), 16)
                        rows_ref[plane // 2, kind, target, into] = jnp.where(
                            ours,
                            own_ref[pair, half, plane // 4, slots, lanes],
                            other_ref[pair, half, plane // 4, slots, lanes],
                        )
            packed_ref[target, :] = scale_ref[pl.ds(pl.multiple_of(pair * 256 + source, 16), 16), :]
            return carry

        lax.fori_loop(0, counts[sequence], move, 0)

    def clear(n, carry):
        target = pl.ds(pl.multiple_of(n * 16, 16), 16)
        for part in range(PARTS):
            for kind in range(2):
                rows_ref[part, kind, target, :] = jnp.zeros((16, 512), BF16)
        packed_ref[target, :] = jnp.zeros((16, 128), F32)
        return carry

    limit = jnp.int32(STEPS[-1] // 16)
    for step in STEPS[-2::-1]:
        limit = jnp.where(starts[4] <= step // 16, step // 16, limit)
    lax.fori_loop(starts[4], limit, clear, 0)

    infac = jnp.zeros((512, 64), F32)
    for plane in range(16):
        in_rows = jnp.concatenate(
            [in_ref[(half * 16 + plane) * 128 : (half * 16 + plane) * 128 + 128, :] for half in range(2)], axis=0
        )
        infac += jnp.dot(
            rows_ref[plane // 2, 0, :, plane % 2 * 256 : plane % 2 * 256 + 256], in_rows, preferred_element_type=F32
        )
    row = lax.broadcasted_iota(jnp.int32, (64, 64), 0)
    column = lax.broadcasted_iota(jnp.int32, (64, 64), 1)
    even_first = (row == jnp.where(column < 32, 2 * column, 2 * column - 63)).astype(F32)
    infac = jnp.dot(infac, even_first, precision=lax.Precision.HIGHEST, preferred_element_type=F32)
    first = lax.broadcasted_iota(jnp.int32, (512, 64), 0) < starts[2] * 16
    infac_ref[...] = jnp.concatenate([jnp.where(first, infac, 0.0), jnp.where(first, 0.0, infac)], axis=1)


def order(place, own, other, in_proj, scale):
    here = pl.BlockSpec(memory_space=pltpu.VMEM)
    return pl.pallas_call(
        order_kernel,
        in_specs=[pl.BlockSpec(memory_space=pltpu.SMEM), here, here, here, here],
        out_specs=[here, here, here],
        out_shape=[
            jax.ShapeDtypeStruct((PARTS, 2, 512, 512), BF16),
            jax.ShapeDtypeStruct((512, 128), F32),
            jax.ShapeDtypeStruct((512, 128), F32),
        ],
        compiler_params=pltpu.CompilerParams(vmem_limit_bytes=24 * MIB),
        cost_estimate=pl.CostEstimate(flops=2 * 512 * 4096 * 64, bytes_accessed=17 * MIB, transcendentals=0),
    )(place, own, other, in_proj, scale)


def layer_kernel(
    place, rows_ref, weight_ref, infac_ref, scale_ref, out_ref, pair_ref, rows, weights, pre, back, sems
):
    def run(count):
        some = slice(0, count)
        copies = [
            (
                pltpu.make_async_copy(weight_ref.at[pl.ds(part * 512, 512), :], weights.at[part], sems.at[0, part]),
                pltpu.make_async_copy(rows_ref.at[part, :, some, :], rows.at[part, :, some, :], sems.at[1, part]),
            )
            for part in range(PARTS)
        ]
        for both in copies:
            for copy in both:
                copy.start()
        for part in range(PARTS):
            for copy in copies[part]:
                copy.wait()
            one = jnp.dot(rows[part, 0, some], weights[part, :, :512], preferred_element_type=F32)
            two = jnp.dot(rows[part, 1, some], weights[part, :, 512:], preferred_element_type=F32)
            if part:
                pre[some, :] += one
                back[some, :] += two
            else:
                pre[some, :] = one
                back[some, :] = two
        gate = pre[some, :256]
        sig = jax.nn.sigmoid(gate)
        slope = sig * (1.0 + gate * (1.0 - sig))
        grad = (scale_ref[some, :1] * back[some, :] * pre[some, 256:] * slope).astype(BF16)
        out = jnp.dot(grad, out_ref[...], preferred_element_type=F32)
        mats = lax.dot_general(
            infac_ref[some, :], out, (((0,), (0,)), ((), ())),
            precision=lax.Precision.HIGHEST, preferred_element_type=F32,
        )
        lane = lax.broadcasted_iota(jnp.int32, (32, 128), 1)
        for pair in range(2):
            mat = mats[pair * 64 : pair * 64 + 64]
            pair_ref[pair] = jnp.where(lane < 64, mat[:32], mat[32:]).astype(BF16)

    total = live_blocks(place)[1][4] * 16
    for below, step in zip((-1,) + STEPS, STEPS):
        pl.when(jnp.logical_and(total > below, total <= step))(lambda step=step: run(step))


def layer(place, rows, weights, infac, scale, out_twice):
    here = pl.BlockSpec(memory_space=pltpu.VMEM)
    there = pl.BlockSpec(memory_space=pl.ANY)
    rows = pltpu.with_memory_space_constraint(rows, pltpu.HBM)
    weights = pltpu.with_memory_space_constraint(weights, pltpu.HBM)
    return pl.pallas_call(
        layer_kernel,
        in_specs=[pl.BlockSpec(memory_space=pltpu.SMEM), there, there, here, here, here],
        out_specs=here,
        out_shape=jax.ShapeDtypeStruct((2, 32, 128), BF16),
        scratch_shapes=[
            pltpu.VMEM((PARTS, 2, 512, 512), BF16),
            pltpu.VMEM((PARTS, 512, 768), BF16),
            pltpu.VMEM((512, 512), F32),
            pltpu.VMEM((512, 256), F32),
            pltpu.SemaphoreType.DMA((2, PARTS)),
        ],
        compiler_params=pltpu.CompilerParams(vmem_limit_bytes=40 * MIB),
        cost_estimate=pl.CostEstimate(flops=2 * 512 * 4096 * 768, bytes_accessed=15 * MIB, transcendentals=131072),
    )(place, rows, weights, infac, scale, out_twice)


def per_device(
    tokens, upstream, rewards, lengths, gate_weight, up_weight, down_weight, in_proj, out_proj, test_grads
):
    xh, z, core = lax.axis_index("xh"), lax.axis_index("z"), lax.axis_index("c")
    place = jnp.stack([xh, z, core]).astype(jnp.int32)
    swap = [(0, 1), (1, 0)]

    theirs = lax.ppermute(pack(True, place, gate_weight, up_weight, down_weight), "xh", swap)
    mine = pack(False, place, gate_weight, up_weight, down_weight)
    block = lax.dynamic_update_slice(mine, theirs[None], (1 - xh, 0, 0))
    weights = lax.all_gather(block, "z").reshape(4096, 768)

    acts = jnp.concatenate([tokens, upstream], axis=0) + theirs[0, 0] * 0
    own = lax.all_to_all(jnp.broadcast_to(acts[None], (16, 512, 256)), PLANE, 0, 0).reshape(2, 2, 4, 512, 256)
    other = lax.ppermute(own, "c", swap)

    coef = jax.nn.sigmoid(rewards[0, 1] - rewards[0, 0])
    known = jnp.pad(jnp.stack([coef, lengths[0, 0].astype(F32), lengths[0, 1].astype(F32)]), (0, 125))[None]
    known_other = lax.ppermute(known, "xh", swap)
    known = jnp.where(xh == 0, jnp.concatenate([known, known_other]), jnp.concatenate([known_other, known]))
    position = lax.broadcasted_iota(jnp.int32, (2, 2, 128), 2).astype(F32)
    side = lax.broadcasted_iota(jnp.int32, (2, 2, 128), 1)
    live = (position < known[:, 1:3, None]).astype(F32)
    scale = known[:, :1, None] * jnp.where(side == 1, 1.0, -1.0).astype(F32) * live
    scale = jnp.broadcast_to(scale.reshape(512, 1), (512, 128))
    ready = jnp.concatenate([place, known[:, 1:3].reshape(4).astype(jnp.int32)])

    out_half = jnp.where(xh == 0, out_proj[:256], out_proj[256:])
    out_twice = jnp.concatenate([out_half, out_half], axis=1)

    rows, infac, packed = order(ready, own, other, in_proj, scale)
    pairs = layer(ready, rows, weights, infac, packed, out_twice)
    spread = jnp.broadcast_to(pairs[:, None], (2, 16, 32, 128)).reshape(32, 32, 128)
    parts = lax.all_to_all(spread, ("xh",) + TEST, 0, 0)
    flat = jnp.sum(parts.astype(F32), axis=0).astype(BF16).reshape(1, 4096)
    return lax.dot_general(flat, test_grads, (((1,), (1,)), ((), ())), preferred_element_type=F32)


def solution(mesh):
    fine = Mesh(mesh.devices.reshape(SIZES), NAMES)
    placed = (
        P(DP, TEST),
        P(DP, TEST),
        P(DP, None),
        P(DP, None),
        P(DP, TEST),
        P(DP, TEST),
        P(TEST, DP),
        P(),
        P(TEST, None),
        P(TEST, None),
    )
    return jax.shard_map(per_device, mesh=fine, in_specs=placed, out_specs=P(DP, TEST), check_vma=False)
```
